128 devices in a mesh: pb: 16 (over z, y), ka: 8 (over x, core).
Axes of the slice: x: 4, y: 4, z: 4, core: 2. Of those that a mesh axis runs over, the one named last changes fastest.
Arguments:
- queries: bfloat16 [16384, 256], P('pb'), may hold values from -4.5 to 4.5
- keys: bfloat16 [16384, 256], P('ka'), may hold values from -4.5 to 4.5
- values: bfloat16 [16384, 256], P('ka'), may hold values from -6 to 6
- grad_out: bfloat16 [16384, 256], P('pb'), may hold values from -384 to 384
- key_lengths: int32 [8], P('ka'), may hold values from 1024 to 2048, as said below
Outputs:
- grad_queries: float32 [16384, 256], P(('pb', 'ka'))
- grad_keys: float32 [16384, 256], P(('ka', 'pb'))
- grad_values: float32 [16384, 256], P(('ka', 'pb'))
The draws below stay inside these ranges and needn't reach their ends.
Inputs may be any that keep to these rules, and one draw needn't show every extreme that they name: Key block b holds key_lengths[b] valid keys at its start, the rest are padding.
All inputs are finite; a program needn't handle non-finite values.
Results may differ from the reference program's by a relative error of at most 0.0035.
Values sent between devices are 32-bit elements; how exact they have to be, the bound alone decides.
A program may use at most 64 MiB of HBM per device.

```python
import jax
import jax.numpy as jnp
from jax import lax

HD = 128
HEADS = 2
K_DEV = 2048
LEN = 16384


def drawn_pair(key):
    feature_width = HEADS * HD
    query_table = jnp.clip(jax.random.normal(jax.random.fold_in(key, 11), (LEN, feature_width), jnp.float32), -4.5, 4.5)
    key_table = jnp.clip(jax.random.normal(jax.random.fold_in(key, 12), (LEN, feature_width), jnp.float32), -4.5, 4.5)
    return (query_table, key_table)


def draw_queries(key, part):
    return drawn_pair(key)[0].astype(jnp.bfloat16)


def draw_keys(key, part):
    return drawn_pair(key)[1].astype(jnp.bfloat16)


def draw_key_lengths(key, part):
    block_total = LEN // K_DEV
    lengths_drawn = jax.random.randint(jax.random.fold_in(key, 21), (block_total,), K_DEV // 2, K_DEV + 1)
    position = jax.random.randint(jax.random.fold_in(key, 22), (), 0, block_total)
    lengths_drawn = lengths_drawn.at[position].set(K_DEV)
    lengths_drawn = lengths_drawn.at[(position + 1) % block_total].set(K_DEV // 2)
    return lengths_drawn.astype(jnp.int32)


def steps_of(rng, extent, cuts, smallest, top_value):
    factor_of, own = 1.0, jax.random.fold_in(rng, 6)
    for dim, parts in cuts:
        steps = jnp.exp(jax.random.uniform(jax.random.fold_in(own, dim), (parts,), jnp.float32, smallest / len(cuts), top_value / len(cuts)))
        factor_of = factor_of * jnp.repeat(steps, extent[dim] // parts).reshape([-1 if axis == dim else 1 for axis in range(len(extent))])
    return factor_of


def bell_draw(key, shape, scale, limit, split=(), kind=jnp.bfloat16):
    drawn = jax.random.normal(key, shape, jnp.float32) * scale
    if len(split) > 0:
        drawn = steps_of(key, shape, split, -0.22, 0.18) * drawn
    return jnp.clip(drawn, min=-limit, max=limit).astype(kind)


def setup_inputs(seed: int = 0) -> dict:
    arg_keys = jax.random.split(jax.random.key(seed), 6)
    return {
        "queries": draw_queries(jax.random.fold_in(arg_keys[5], 71), 0),
        "keys": draw_keys(jax.random.fold_in(arg_keys[5], 71), 0),
        "values": bell_draw(arg_keys[2], (LEN, HEADS * HD), 1.0, 6.0, ((0, 8),)),
        "grad_out": bell_draw(arg_keys[3], (LEN, HEADS * HD), 64.0, 384.0, ((0, 16),)),
        "key_lengths": draw_key_lengths(jax.random.fold_in(arg_keys[5], 71), 0),
    }


relax_weight = 0.9


def rounded(values_in):
    return lax.optimization_barrier(values_in.astype(jnp.bfloat16)).astype(jnp.float32)


def reference(queries, keys, values, grad_out, key_lengths):
    total = queries.shape[0]
    feature_width = queries.shape[1]
    head_count = HEADS
    scaling = HD ** -0.5
    block_rows = min(1024, total)
    block_count = total // block_rows
    query_blocks = queries.astype(jnp.float32).reshape(block_count, block_rows, head_count, HD)
    grad_blocks = grad_out.astype(jnp.float32).reshape(block_count, block_rows, head_count, HD)
    key_heads = keys.astype(jnp.float32).reshape(total, head_count, HD)
    value_heads = values.astype(jnp.float32).reshape(total, head_count, HD)
    columns = jnp.arange(total, dtype=jnp.int32)
    is_valid = (columns % K_DEV) < key_lengths[columns // K_DEV]

    def scores(query_block):
        return jnp.einsum("bhd,khd->hbk", query_block, key_heads) * scaling

    def masked_exp(logits):
        return jnp.where(is_valid, jnp.exp(logits), jnp.float32(0.0))

    def to_blocks(vector):
        return vector.reshape(head_count, block_count, block_rows).transpose(1, 0, 2)

    def from_blocks(stacked):
        return stacked.transpose(1, 0, 2).reshape(head_count, total)

    def row_potential(col_pot):
        def one_block(query_block):
            logits = jnp.where(is_valid, scores(query_block) + col_pot[:, None, :], -jnp.inf)
            peak = jnp.max(logits, axis=-1)
            mass = jnp.sum(jnp.exp(logits - peak[..., None]), axis=-1)
            return -(peak + jnp.log(mass))
        return from_blocks(lax.map(one_block, query_blocks))

    def col_potential(row_pot):
        def one_block(inputs):
            query_block, pot_block = inputs
            logits = scores(query_block) + pot_block[:, :, None]
            peak = jnp.max(logits, axis=1)
            return peak, jnp.sum(jnp.exp(logits - peak[:, None, :]), axis=1)
        peaks, masses = lax.map(one_block, (query_blocks, to_blocks(row_pot)))
        highest = jnp.max(peaks, axis=0)
        mass = jnp.sum(masses * jnp.exp(peaks - highest), axis=0)
        return -relax_weight * (highest + jnp.log(mass))

    zero_cols = jnp.zeros((head_count, total), jnp.float32)
    row_first = row_potential(zero_cols)
    col_first = col_potential(row_first)
    row_second = row_potential(col_first)
    col_second = col_potential(row_second)

    def first_pass(carry, inputs):
        col_acc, value_acc = carry
        query_block, grad_block, pot_block = inputs
        logits = scores(query_block)
        probs = masked_exp(logits + pot_block[:, :, None] + col_second[:, None, :])
        grad_probs = jnp.einsum("bhd,khd->hbk", grad_block, value_heads)
        product = probs * grad_probs
        value_acc = value_acc + jnp.einsum("hbk,bhd->khd", rounded(probs), grad_block)
        return (col_acc + jnp.sum(product, axis=1), value_acc), jnp.sum(product, axis=-1)

    init_values = jnp.zeros((total, head_count, HD), jnp.float32)
    (col_adjoint, value_acc), row_parts = lax.scan(first_pass, (zero_cols, init_values), (query_blocks, grad_blocks, to_blocks(row_second)))
    row_adjoint = from_blocks(row_parts)

    def second_pass(inputs):
        query_block, pot_block = inputs
        weights = masked_exp(scores(query_block) + pot_block[:, :, None] + col_second[:, None, :] / relax_weight)
        return jnp.sum(weights * col_adjoint[:, None, :], axis=-1)

    coupled = from_blocks(lax.map(second_pass, (query_blocks, to_blocks(row_second))))
    row_second_adj = row_adjoint - relax_weight * coupled

    def third_pass(inputs):
        query_block, adj_block, pot_block = inputs
        weights = masked_exp(scores(query_block) + col_first[:, None, :] + pot_block[:, :, None])
        return -jnp.sum(weights * adj_block[:, :, None], axis=1)

    col_first_adj = jnp.sum(lax.map(third_pass, (query_blocks, to_blocks(row_second_adj), to_blocks(row_second))), axis=0)

    def fourth_pass(inputs):
        query_block, pot_block = inputs
        weights = masked_exp(scores(query_block) + pot_block[:, :, None] + col_first[:, None, :] / relax_weight)
        return -relax_weight * jnp.sum(weights * col_first_adj[:, None, :], axis=-1)

    row_first_adj = from_blocks(lax.map(fourth_pass, (query_blocks, to_blocks(row_first))))

    def fifth_pass(key_acc, inputs):
        query_block, grad_block, first_block, second_block, second_adj, first_adj = inputs
        logits = scores(query_block)
        probs = masked_exp(logits + second_block[:, :, None] + col_second[:, None, :])
        grad_probs = jnp.einsum("bhd,khd->hbk", grad_block, value_heads)
        grad_logits = probs * grad_probs
        grad_logits = grad_logits - relax_weight * col_adjoint[:, None, :] * masked_exp(logits + second_block[:, :, None] + col_second[:, None, :] / relax_weight)
        grad_logits = grad_logits - second_adj[:, :, None] * masked_exp(logits + col_first[:, None, :] + second_block[:, :, None])
        grad_logits = grad_logits - relax_weight * col_first_adj[:, None, :] * masked_exp(logits + first_block[:, :, None] + col_first[:, None, :] / relax_weight)
        grad_logits = grad_logits - first_adj[:, :, None] * masked_exp(logits + first_block[:, :, None])
        rounded_logits = rounded(grad_logits)
        query_grad = jnp.einsum("hbk,khd->bhd", rounded_logits, key_heads) * scaling
        key_acc = key_acc + jnp.einsum("hbk,bhd->khd", rounded_logits, query_block) * scaling
        return key_acc, query_grad

    key_acc, query_parts = lax.scan(fifth_pass, init_values, (query_blocks, grad_blocks, to_blocks(row_first), to_blocks(row_second), to_blocks(row_second_adj), to_blocks(row_first_adj)))
    grad_queries = query_parts.reshape(total, feature_width)
    grad_keys = key_acc.reshape(total, feature_width)
    grad_values = value_acc.reshape(total, feature_width)
    return (grad_queries, grad_keys, grad_values)
```

```python
import functools

import jax
import jax.numpy as jnp
from jax import lax
from jax.experimental import pallas as pl
from jax.experimental.pallas import tpu as pltpu
from jax.sharding import PartitionSpec as P

HD = 128
HEADS = 2
LANES = 128
RELAX = 0.9
LOG2E = 1.4426950408889634
MESH = pl.DeviceIdType.MESH
F32 = jnp.float32
BF16 = jnp.bfloat16
NEG = -1e30


def far(n):
    return min(n, 4 - n)


KA_OFFS = sorted(
    [(a, c) for a in range(4) for c in range(2) if a or c], key=lambda o: -far(o[0])
)
PB_OFFS = sorted(
    [(a, b) for a in range(4) for b in range(4) if a or b], key=lambda o: -far(o[0]) - far(o[1])
)
HOPS = (2, 1, 3)


def kernel(
    rows, cols, len_ref, q_hbm, k_hbm, v_hbm, o_hbm, gq_ref, gk_ref, gv_ref,
    q, k, v, o, qt, ot, kk, dd, bb, ra, rb, rw, ry, cv, cp,
    kab, pbb, dv, dk, dq, s1, p1, s2, sq,
    in_sem, ka_s, ka_r, pb_s, pb_r, s1_s, s1_r, s2_s, s2_r, sq_s, sq_r,
):
    tiles = cols // LANES
    blocks = rows // LANES
    groups = rows // 8
    pb, ka = lax.axis_index("pb"), lax.axis_index("ka")
    z, y = pb // 4, lax.rem(pb, 4)
    xx, cc = ka // 2, lax.rem(ka, 2)

    def ka_peer(off):
        return (pb, lax.rem(xx + off[0], 4) * 2 + lax.rem(cc + off[1], 2))

    def pb_peer(off):
        return (lax.rem(z + off[0], 4) * 4 + lax.rem(y + off[1], 4), ka)

    loads = [
        pltpu.make_async_copy(src, dst, in_sem.at[n])
        for n, (src, dst) in enumerate(((q_hbm, q), (k_hbm, k), (v_hbm, v), (o_hbm, o)))
    ]
    for copy in loads:
        copy.start()
    barrier = pltpu.get_barrier_semaphore()
    for off in KA_OFFS:
        pl.semaphore_signal(barrier, inc=1, device_id=ka_peer(off), device_id_type=MESH)
    for off in PB_OFFS:
        pl.semaphore_signal(barrier, inc=1, device_id=pb_peer(off), device_id_type=MESH)

    def ka_copies(r, h):
        return [
            pltpu.make_async_remote_copy(
                src_ref=kab.at[r, h, 0], dst_ref=kab.at[r, h, n + 1],
                send_sem=ka_s.at[r, h, n], recv_sem=ka_r.at[r, h, n],
                device_id=ka_peer(off), device_id_type=MESH,
            )
            for n, off in enumerate(KA_OFFS)
        ]

    def pb_copies(r, h):
        return [
            pltpu.make_async_remote_copy(
                src_ref=pbb.at[r, h, 0], dst_ref=pbb.at[r, h, n + 1],
                send_sem=pb_s.at[r, h, n], recv_sem=pb_r.at[r, h, n],
                device_id=pb_peer(off), device_id_type=MESH,
            )
            for n, off in enumerate(PB_OFFS)
        ]

    def start(copies):
        for copy in copies:
            copy.start()

    def arrive(copies):
        for copy in copies:
            copy.wait_recv()

    def drain(copies):
        for copy in copies:
            copy.wait_send()

    eye = lax.broadcasted_iota(jnp.int32, (LANES, LANES), 0) == lax.broadcasted_iota(
        jnp.int32, (LANES, LANES), 1
    )
    position = lax.broadcasted_iota(jnp.int32, (tiles, LANES), 0) * LANES + lax.broadcasted_iota(
        jnp.int32, (tiles, LANES), 1
    )
    valid = position < len_ref[0]

    def to_lanes(column):
        return jnp.sum(jnp.where(eye, column, 0.0), axis=0, keepdims=True)

    def spread_rows(compact, ref, h):
        for b in range(blocks):
            column = jnp.sum(jnp.where(eye, compact[b : b + 1, :], 0.0), axis=1, keepdims=True)
            ref[h, b * LANES : (b + 1) * LANES, :] = jnp.broadcast_to(column, (LANES, LANES))

    def spread_cols(compact, n, h):
        for t in range(tiles):
            cv[h, n, :, t * LANES : (t + 1) * LANES] = jnp.broadcast_to(
                compact[t : t + 1, :], (8, LANES)
            )

    def pack_cols(line, ref):
        for t in range(tiles):
            ref[t : t + 1, :] = line[:, t * LANES : (t + 1) * LANES]

    def wide(column):
        return jnp.concatenate([column] * tiles, axis=1)

    def fold(block, op):
        parts = [block[:, t * LANES : (t + 1) * LANES] for t in range(tiles)]
        while len(parts) > 1:
            parts = [op(a, b) for a, b in zip(parts[::2], parts[1::2])]
        return parts[0]

    def group(g):
        return pl.ds(pl.multiple_of(g * 8, 8), 8)

    def log2(x):
        return jnp.log(x) * LOG2E

    BIAS, RHO, PROB, BETA, GAMMA, SIGMA = range(6)
    LOGC, KAPPA = range(2)
    spread_cols(jnp.where(valid, 0.0, NEG), BIAS, 0)

    def head(h):
        return slice(h * HD, (h + 1) * HD)

    mm = 256

    def product(a, b, h, i):
        sl = pl.ds(pl.multiple_of(i * mm, mm), mm)
        return sl, lax.dot_general(
            a[sl, head(h)], b[:, head(h)], (((1,), (1,)), ((), ())), preferred_element_type=F32
        )

    def scores(h):
        def body(i, c):
            sl, s = product(q, k, h, i)
            kk[h, sl, :] = s * (HD**-0.5 * LOG2E) + cv[0, BIAS, 0:1, :]
            return c

        lax.fori_loop(0, rows // mm, body, 0)

        def sweep(g, c):
            sl = group(g)
            s = kk[h, sl, :]
            peak = fold(s, jnp.maximum)
            ra[h, sl, :] = peak
            rb[h, sl, :] = fold(jnp.exp2(s - wide(peak)), jnp.add)
            return c

        lax.fori_loop(0, groups, sweep, 0, unroll=4)
        for b in range(blocks):
            sl = slice(b * LANES, (b + 1) * LANES)
            peak = ra[h, sl, :]
            highest = jnp.max(peak, axis=1, keepdims=True)
            mass = jnp.sum(rb[h, sl, :] * jnp.exp2(peak - highest), axis=1, keepdims=True)
            kab[0, h, 0, 0, b : b + 1, :] = to_lanes(highest)
            kab[0, h, 0, 1, b : b + 1, :] = to_lanes(mass)

    loads[0].wait()
    loads[1].wait()
    scores(0)
    pl.semaphore_wait(barrier, len(KA_OFFS) + len(PB_OFFS))
    start(ka_copies(0, 0))
    scores(1)
    start(ka_copies(0, 1))

    loads[2].wait()
    loads[3].wait()
    for h in range(HEADS):

        def body(i, c):
            sl, s = product(o, v, h, i)
            dd[h, sl, :] = s
            return c

        lax.fori_loop(0, rows // mm, body, 0)
    for h in range(HEADS):
        qt[h] = q[:, head(h)].astype(F32).T.astype(BF16)
        ot[h] = o[:, head(h)].astype(F32).T.astype(BF16)

    def merge(parts):
        highest = parts[0][0]
        for m, _ in parts[1:]:
            highest = jnp.maximum(highest, m)
        mass = sum(s * jnp.exp2(m - highest) for m, s in parts)
        return highest + log2(mass)

    def first_columns(h):
        pot = -merge([(kab[0, h, n, 0], kab[0, h, n, 1]) for n in range(8)])
        spread_rows(pot, rw, h)

        def peaks(g, acc):
            sl = group(g)
            return jnp.maximum(acc, kk[h, sl, :] + wide(rw[h, sl, :]))

        acc = lax.fori_loop(0, groups, peaks, jnp.full((8, cols), NEG, F32), unroll=4)
        peak = jnp.maximum(jnp.max(acc, axis=0, keepdims=True), -1e4)
        lift = jnp.broadcast_to(peak, (8, cols))

        def masses(g, acc):
            sl = group(g)
            e = jnp.exp2(kk[h, sl, :] + wide(rw[h, sl, :]) - lift)
            kk[h, sl, :] = e
            return acc + e

        acc = lax.fori_loop(0, groups, masses, jnp.zeros((8, cols), F32), unroll=4)
        pack_cols(peak, pbb.at[0, h, 0, 0])
        pack_cols(jnp.sum(acc, axis=0, keepdims=True), pbb.at[0, h, 0, 1])

    for h in range(HEADS):
        arrive(ka_copies(0, h))
        first_columns(h)
        start(pb_copies(0, h))

    def row_sums(n, r, h):
        x = cv[h, n]

        def body(g, c):
            sl = group(g)
            ra[h, sl, :] = fold(kk[h, sl, :] * x, jnp.add)
            return c

        lax.fori_loop(0, groups, body, 0, unroll=4)
        pack_rows(r, h)

    def pack_rows(r, h):
        for b in range(blocks):
            column = jnp.sum(ra[h, b * LANES : (b + 1) * LANES, :], axis=1, keepdims=True)
            kab[r, h, 0, 0, b : b + 1, :] = to_lanes(column)

    def row_total(r, h):
        return sum(kab[r, h, n, 0] for n in range(8))

    def col_total(r, h, n):
        return sum(pbb[r, h, m, n] for m in range(16))

    for h in range(HEADS):
        arrive(pb_copies(0, h))
        logc = merge([(pbb[0, h, n, 0], pbb[0, h, n, 1]) for n in range(16)])
        logc = jnp.where(valid, logc, 0.0)
        kappa = jnp.where(valid, jnp.exp2(pbb[0, h, 0, 0] - logc), 0.0)
        cp[h, LOGC] = logc
        cp[h, KAPPA] = kappa
        spread_cols(kappa * jnp.exp2((1.0 - RELAX) * logc), RHO, h)
        spread_cols(kappa * jnp.exp2(logc), SIGMA, h)
        row_sums(RHO, 1, h)
        start(ka_copies(1, h))

    def second_columns(h):
        spread_rows(1.0 / row_total(1, h), rw, h)

        def body(g, accs):
            sl = group(g)
            kw = kk[h, sl, :] * wide(rw[h, sl, :])
            return accs[0] + kw, accs[1] + kw * dd[h, sl, :]

        zero = jnp.zeros((8, cols), F32)
        mass, adjoint = lax.fori_loop(0, groups, body, (zero, zero), unroll=2)
        kappa = cp[h, KAPPA]
        pack_cols(jnp.sum(mass, axis=0, keepdims=True), pbb.at[1, h, 0, 0])
        pack_cols(jnp.sum(adjoint, axis=0, keepdims=True), pbb.at[1, h, 0, 1])
        pbb[1, h, 0, 0] = pbb[1, h, 0, 0] * kappa
        pbb[1, h, 0, 1] = pbb[1, h, 0, 1] * kappa

    for h in range(HEADS):
        arrive(ka_copies(1, h))
        second_columns(h)
        start(pb_copies(1, h))

    def second_rows(h):
        mass = jnp.where(valid, col_total(1, h, 0), 1.0)
        kappa = cp[h, KAPPA]
        power = jnp.exp2((1.0 - RELAX) * cp[h, LOGC] - RELAX * log2(mass))
        spread_cols(kappa * power, PROB, h)
        spread_cols(RELAX * power * col_total(1, h, 1) * kappa / mass, BETA, h)

        def body(g, c):
            sl = group(g)
            t = (kk[h, sl, :] * wide(rw[h, sl, :])) * (dd[h, sl, :] * cv[h, PROB] - cv[h, BETA])
            dd[h, sl, :] = t
            ra[h, sl, :] = fold(t, jnp.add)
            return c

        lax.fori_loop(0, groups, body, 0, unroll=2)
        pack_rows(2, h)

    for h in range(HEADS):
        arrive(pb_copies(1, h))
        second_rows(h)
        start(ka_copies(2, h))

    def rs_first(w, h, part):
        copies = []
        for a in HOPS:
            ty, tz = lax.rem(y + a, 4), lax.rem(z + a, 4)
            if h == 0:
                src, dev = part.at[h, :, ty], (z * 4 + ty, ka)
            else:
                src, dev = part.at[h, tz], (tz * 4 + y, ka)
            copies.append(
                pltpu.make_async_remote_copy(
                    src_ref=src, dst_ref=s1.at[w, h, a - 1],
                    send_sem=s1_s.at[w, h, a - 1], recv_sem=s1_r.at[w, h, a - 1],
                    device_id=dev, device_id_type=MESH,
                )
            )
        return copies

    def rs_second(w, h):
        copies = []
        for a in HOPS:
            ty, tz = lax.rem(y + a, 4), lax.rem(z + a, 4)
            t, dev = (tz, (tz * 4 + y, ka)) if h == 0 else (ty, (z * 4 + ty, ka))
            copies.append(
                pltpu.make_async_remote_copy(
                    src_ref=p1.at[w, h, t], dst_ref=s2.at[w, h, a - 1],
                    send_sem=s2_s.at[w, h, a - 1], recv_sem=s2_r.at[w, h, a - 1],
                    device_id=dev, device_id_type=MESH,
                )
            )
        return copies

    def rs_middle(w, h, part):
        arrive(rs_first(w, h, part))
        copies = rs_second(w, h)
        for n, a in enumerate(HOPS + (0,)):
            t = lax.rem((z if h == 0 else y) + a, 4)

            def body(i, c):
                sl = pl.ds(pl.multiple_of(i * 32, 32), 32)
                own = part[h, t, y, sl] if h == 0 else part[h, z, t, sl]
                p1[w, h, t, sl] = own + s1[w, h, 0, t, sl] + s1[w, h, 1, t, sl] + s1[w, h, 2, t, sl]
                return c

            lax.fori_loop(0, 4, body, 0)
            if a:
                copies[n].start()

    def rs_last(w, h, scale, out):
        arrive(rs_second(w, h))
        t = z if h == 0 else y
        total = (p1[w, h, t] + s2[w, h, 0]) + (s2[w, h, 1] + s2[w, h, 2])
        out[:, head(h)] = total.T * scale

    def by_columns(lhs, part, h):
        def body(n, c):
            sl = pl.ds(pl.multiple_of(n * 256, 256), 256)
            res = jnp.dot(lhs[h], bb[:, sl], preferred_element_type=F32)
            part[h, n // 2, 2 * lax.rem(n, 2)] = res[:, :LANES]
            part[h, n // 2, 2 * lax.rem(n, 2) + 1] = res[:, LANES:]
            return c

        lax.fori_loop(0, cols // 256, body, 0)

    def value_part(h):
        def body(g, c):
            sl = pl.ds(pl.multiple_of(g * 16, 16), 16)
            w = rw[h, sl, :]
            prob = (kk[h, sl, :] * wide(w)) * cv[h, PROB, 0:1, :]
            bb[sl, :] = prob.astype(BF16)
            return c

        lax.fori_loop(0, rows // 16, body, 0, unroll=2)
        by_columns(ot, dv, h)

    for h in range(HEADS):
        value_part(h)

    def first_adjoint(h):
        total = row_total(2, h)
        spread_rows(total, ry, h)

        def body(g, acc):
            sl = group(g)
            yw = ry[h, sl, :] * rw[h, sl, :]
            ry[h, sl, :] = yw
            return acc + kk[h, sl, :] * wide(yw)

        acc = lax.fori_loop(0, groups, body, jnp.zeros((8, cols), F32), unroll=4)
        pack_cols(jnp.sum(acc, axis=0, keepdims=True), pbb.at[2, h, 0, 0])
        pbb[2, h, 0, 0] = pbb[2, h, 0, 0] * cp[h, KAPPA]

    for h in range(HEADS):
        arrive(ka_copies(2, h))
        first_adjoint(h)
        start(pb_copies(2, h))
    for h in range(HEADS):
        start(rs_first(0, h, dv))

    for h in range(HEADS):
        arrive(pb_copies(2, h))
        adj = -jnp.exp2((1.0 - RELAX) * cp[h, LOGC]) * col_total(2, h, 0)
        spread_cols(RELAX * cp[h, KAPPA] * adj, GAMMA, h)
        row_sums(GAMMA, 3, h)
        start(ka_copies(3, h))

    for h in range(HEADS):

        def body(g, c):
            sl = group(g)
            yw = wide(ry[h, sl, :])
            dd[h, sl, :] = dd[h, sl, :] - kk[h, sl, :] * (yw * cv[h, RHO] + cv[h, GAMMA])
            return c

        lax.fori_loop(0, groups, body, 0, unroll=2)

    def sq_copies(h):
        copies = []
        for n, off in enumerate(KA_OFFS):
            dev = ka_peer(off)
            copies.append(
                pltpu.make_async_remote_copy(
                    src_ref=dq.at[h, dev[1]], dst_ref=sq.at[h, n],
                    send_sem=sq_s.at[h, n], recv_sem=sq_r.at[h, n],
                    device_id=dev, device_id_type=MESH,
                )
            )
        return copies

    for h in range(HEADS):
        arrive(ka_copies(3, h))
        spread_rows(-row_total(3, h), ry, h)

        def body(g, c):
            sl = pl.ds(pl.multiple_of(g * 16, 16), 16)
            zw = wide(ry[h, sl, :])
            bb[sl, :] = (dd[h, sl, :] - kk[h, sl, :] * (zw * cv[h, SIGMA, 0:1, :])).astype(BF16)
            return c

        lax.fori_loop(0, rows // 16, body, 0, unroll=2)
        by_columns(qt, dk, h)
        start(rs_first(1, h, dk))

        def body(i, c):
            sl = pl.ds(pl.multiple_of(i * mm, mm), mm)
            res = jnp.dot(bb[sl, :], k[:, head(h)], preferred_element_type=F32)
            for n in range(mm // LANES):
                dq[h, i * (mm // LANES) + n] = res[n * LANES : (n + 1) * LANES]
            return c

        lax.fori_loop(0, rows // mm, body, 0)
        start(sq_copies(h))

    for w, part in ((0, dv), (1, dk)):
        for h in range(HEADS):
            rs_middle(w, h, part)
    for h in range(HEADS):
        rs_last(0, h, 1.0, gv_ref)
    for h in range(HEADS):
        arrive(sq_copies(h))
        total = dq[h, ka]
        for n in range(7):
            total = total + sq[h, n]
        gq_ref[:, head(h)] = total * HD**-0.5
    for h in range(HEADS):
        rs_last(1, h, HD**-0.5, gk_ref)

    for h in range(HEADS):
        for r in range(4):
            drain(ka_copies(r, h))
        for r in range(3):
            drain(pb_copies(r, h))
        for w, part in ((0, dv), (1, dk)):
            drain(rs_first(w, h, part))
            drain(rs_second(w, h))
        drain(sq_copies(h))


def shards(queries, keys, values, grad_out, key_lengths):
    rows, width = queries.shape
    cols = keys.shape[0]
    vmem = lambda *shape: pltpu.VMEM(shape, F32)
    half = lambda *shape: pltpu.VMEM(shape, BF16)
    dma = lambda *shape: pltpu.SemaphoreType.DMA(shape)
    scratch = [
        half(rows, width), half(cols, width), half(cols, width), half(rows, width),
        half(HEADS, HD, rows), half(HEADS, HD, rows),
        vmem(HEADS, rows, cols), vmem(HEADS, rows, cols), half(rows, cols),
        vmem(HEADS, rows, LANES), vmem(HEADS, rows, LANES),
        vmem(HEADS, rows, LANES), vmem(HEADS, rows, LANES),
        vmem(HEADS, 6, 8, cols), vmem(HEADS, 2, cols // LANES, LANES),
        vmem(4, HEADS, 8, 2, rows // LANES, LANES),
        vmem(3, HEADS, 16, 2, cols // LANES, LANES),
        vmem(HEADS, 4, 4, HD, LANES), vmem(HEADS, 4, 4, HD, LANES),
        vmem(HEADS, rows // LANES, LANES, HD),
        vmem(2, HEADS, 3, 4, HD, LANES), vmem(2, HEADS, 4, HD, LANES),
        vmem(2, HEADS, 3, HD, LANES), vmem(HEADS, 7, LANES, HD),
        dma(4), dma(4, HEADS, 7), dma(4, HEADS, 7), dma(3, HEADS, 15), dma(3, HEADS, 15),
        dma(2, HEADS, 3), dma(2, HEADS, 3), dma(2, HEADS, 3), dma(2, HEADS, 3),
        dma(HEADS, 7), dma(HEADS, 7),
    ]
    hbm = pl.BlockSpec(memory_space=pl.ANY)
    here = pl.BlockSpec(memory_space=pltpu.VMEM)
    return pl.pallas_call(
        functools.partial(kernel, rows, cols),
        out_shape=(
            jax.ShapeDtypeStruct((rows // 8, width), F32),
            jax.ShapeDtypeStruct((cols // 16, width), F32),
            jax.ShapeDtypeStruct((cols // 16, width), F32),
        ),
        in_specs=[pl.BlockSpec(memory_space=pltpu.SMEM), hbm, hbm, hbm, hbm],
        out_specs=(here, here, here),
        scratch_shapes=scratch,
        compiler_params=pltpu.CompilerParams(
            collective_id=0, has_side_effects=True, vmem_limit_bytes=60 * 2**20
        ),
        cost_estimate=pl.CostEstimate(
            flops=24 * rows * cols * HD, bytes_accessed=2**22, transcendentals=4 * rows * cols
        ),
    )(key_lengths, queries, keys, values, grad_out)


def solution(mesh):
    placed = (P("pb", None), P("ka", None), P("ka", None), P("pb", None), P("ka"))
    return jax.shard_map(
        shards,
        mesh=mesh,
        in_specs=placed,
        out_specs=(P(("pb", "ka"), None), P(("ka", "pb"), None), P(("ka", "pb"), None)),
        check_vma=False,
    )
```

```python
import functools

import jax
import jax.numpy as jnp
from jax import lax
from jax.experimental import pallas as pl
from jax.experimental.pallas import tpu as pltpu
from jax.sharding import PartitionSpec as P

HD = 128
HEADS = 2
LANES = 128
RELAX = 0.9
LOG2E = 1.4426950408889634
MESH = pl.DeviceIdType.MESH
F32 = jnp.float32
BF16 = jnp.bfloat16
NEG = -1e30


def far(n):
    return min(n, 4 - n)


KA_OFFS = sorted(
    [(a, c) for a in range(4) for c in range(2) if a or c], key=lambda o: -far(o[0])
)
PB_OFFS = sorted(
    [(a, b) for a in range(4) for b in range(4) if a or b], key=lambda o: -far(o[0]) - far(o[1])
)
HOPS = (2, 1, 3)


def kernel(
    rows, cols, len_ref, q_hbm, k_hbm, v_hbm, o_hbm, gq_ref, gk_ref, gv_ref,
    q, k, v, o, qt, ot, kk, dd, bb, ra, rb, rw, ry, cv, cp,
    kab, pbb, dv, dk, dq, s1, p1, s2, sq,
    in_sem, ka_s, ka_r, pb_s, pb_r, s1_s, s1_r, s2_s, s2_r, sq_s, sq_r,
):
    tiles = cols // LANES
    blocks = rows // LANES
    groups = rows // 8
    pb, ka = lax.axis_index("pb"), lax.axis_index("ka")
    z, y = pb // 4, lax.rem(pb, 4)
    xx, cc = ka // 2, lax.rem(ka, 2)

    def ka_peer(off):
        return (pb, lax.rem(xx + off[0], 4) * 2 + lax.rem(cc + off[1], 2))

    def pb_peer(off):
        return (lax.rem(z + off[0], 4) * 4 + lax.rem(y + off[1], 4), ka)

    loads = [
        pltpu.make_async_copy(src, dst, in_sem.at[n])
        for n, (src, dst) in enumerate(((q_hbm, q), (k_hbm, k), (v_hbm, v), (o_hbm, o)))
    ]
    for copy in loads:
        copy.start()
    barrier = pltpu.get_barrier_semaphore()
    for off in KA_OFFS:
        pl.semaphore_signal(barrier, inc=1, device_id=ka_peer(off), device_id_type=MESH)
    for off in PB_OFFS:
        pl.semaphore_signal(barrier, inc=1, device_id=pb_peer(off), device_id_type=MESH)

    def ka_copies(r, h):
        return [
            pltpu.make_async_remote_copy(
                src_ref=kab.at[r, h, 0], dst_ref=kab.at[r, h, n + 1],
                send_sem=ka_s.at[r, h, n], recv_sem=ka_r.at[r, h, n],
                device_id=ka_peer(off), device_id_type=MESH,
            )
            for n, off in enumerate(KA_OFFS)
        ]

    def pb_copies(r, h):
        return [
            pltpu.make_async_remote_copy(
                src_ref=pbb.at[r, h, 0], dst_ref=pbb.at[r, h, n + 1],
                send_sem=pb_s.at[r, h, n], recv_sem=pb_r.at[r, h, n],
                device_id=pb_peer(off), device_id_type=MESH,
            )
            for n, off in enumerate(PB_OFFS)
        ]

    def start(copies):
        for copy in copies:
            copy.start()

    def arrive(copies):
        for copy in copies:
            copy.wait_recv()

    def drain(copies):
        for copy in copies:
            copy.wait_send()

    eye = lax.broadcasted_iota(jnp.int32, (LANES, LANES), 0) == lax.broadcasted_iota(
        jnp.int32, (LANES, LANES), 1
    )
    position = lax.broadcasted_iota(jnp.int32, (tiles, LANES), 0) * LANES + lax.broadcasted_iota(
        jnp.int32, (tiles, LANES), 1
    )
    valid = position < len_ref[0]

    def to_lanes(column):
        return jnp.sum(jnp.where(eye, column, 0.0), axis=0, keepdims=True)

    def spread_rows(compact, ref, h):
        for b in range(blocks):
            column = jnp.sum(jnp.where(eye, compact[b : b + 1, :], 0.0), axis=1, keepdims=True)
            ref[h, b * LANES : (b + 1) * LANES, :] = jnp.broadcast_to(column, (LANES, LANES))

    def spread_cols(compact, n, h):
        for t in range(tiles):
            cv[h, n, :, t * LANES : (t + 1) * LANES] = jnp.broadcast_to(
                compact[t : t + 1, :], (8, LANES)
            )

    def pack_cols(line, ref):
        for t in range(tiles):
            ref[t : t + 1, :] = line[:, t * LANES : (t + 1) * LANES]

    def wide(column):
        return jnp.concatenate([column] * tiles, axis=1)

    def fold(block, op):
        parts = [block[:, t * LANES : (t + 1) * LANES] for t in range(tiles)]
        while len(parts) > 1:
            parts = [op(a, b) for a, b in zip(parts[::2], parts[1::2])]
        return parts[0]

    def group(g):
        return pl.ds(pl.multiple_of(g * 8, 8), 8)

    def log2(x):
        return jnp.log(x) * LOG2E

    BIAS, RHO, PROB, BETA, GAMMA, SIGMA = range(6)
    LOGC, KAPPA = range(2)
    spread_cols(jnp.where(valid, 0.0, NEG), BIAS, 0)

    def head(h):
        return slice(h * HD, (h + 1) * HD)

    def product(a, b, h):
        return lax.dot_general(
            a[:, head(h)], b[:, head(h)], (((1,), (1,)), ((), ())), preferred_element_type=F32
        )

    def scores(h):
        kk[h] = product(q, k, h) * (HD**-0.5 * LOG2E) + cv[0, BIAS, 0:1, :]

        def sweep(g, c):
            sl = group(g)
            s = kk[h, sl, :]
            peak = fold(s, jnp.maximum)
            ra[h, sl, :] = peak
            rb[h, sl, :] = fold(jnp.exp2(s - wide(peak)), jnp.add)
            return c

        lax.fori_loop(0, groups, sweep, 0, unroll=16)
        for b in range(blocks):
            sl = slice(b * LANES, (b + 1) * LANES)
            peak = ra[h, sl, :]
            highest = jnp.max(peak, axis=1, keepdims=True)
            mass = jnp.sum(rb[h, sl, :] * jnp.exp2(peak - highest), axis=1, keepdims=True)
            kab[0, h, 0, 0, b : b + 1, :] = to_lanes(highest)
            kab[0, h, 0, 1, b : b + 1, :] = to_lanes(mass)

    loads[0].wait()
    loads[1].wait()
    scores(0)
    pl.semaphore_wait(barrier, len(KA_OFFS) + len(PB_OFFS))
    start(ka_copies(0, 0))
    scores(1)
    start(ka_copies(0, 1))

    def output_product(h):
        dd[h] = product(o, v, h)

    def merge(parts):
        highest = parts[0][0]
        for m, _ in parts[1:]:
            highest = jnp.maximum(highest, m)
        mass = sum(s * jnp.exp2(m - highest) for m, s in parts)
        return highest + log2(mass)

    def first_columns(h):
        pot = -merge([(kab[0, h, n, 0], kab[0, h, n, 1]) for n in range(8)])
        spread_rows(pot, rw, h)

        def peaks(g, acc):
            sl = group(g)
            return jnp.maximum(acc, kk[h, sl, :] + wide(rw[h, sl, :]))

        acc = lax.fori_loop(0, groups, peaks, jnp.full((8, cols), NEG, F32), unroll=8)
        peak = jnp.maximum(jnp.max(acc, axis=0, keepdims=True), -1e4)
        cv[h, PROB] = jnp.broadcast_to(peak, (8, cols))

        def masses(g, acc):
            sl = pl.ds(pl.multiple_of(g * 32, 32), 32)
            pot = rw[h, sl, :]
            out = []
            for t in range(tiles):
                cs = slice(t * LANES, (t + 1) * LANES)
                e = jnp.exp2(kk[h, sl, cs] + pot - cv[h, PROB, 0:1, cs])
                kk[h, sl, cs] = e
                out.append(acc[:, cs] + ((e[:8] + e[8:16]) + (e[16:24] + e[24:])))
            return jnp.concatenate(out, axis=1)

        acc = lax.fori_loop(0, rows // 32, masses, jnp.zeros((8, cols), F32))
        pack_cols(peak, pbb.at[0, h, 0, 0])
        pack_cols(jnp.sum(acc, axis=0, keepdims=True), pbb.at[0, h, 0, 1])

    for h in range(HEADS):
        arrive(ka_copies(0, h))
        first_columns(h)
        start(pb_copies(0, h))

    def row_sums(n, r, h):
        x = cv[h, n]

        def body(g, c):
            sl = group(g)
            ra[h, sl, :] = fold(kk[h, sl, :] * x, jnp.add)
            return c

        lax.fori_loop(0, groups, body, 0, unroll=8)
        pack_rows(r, h)

    def pack_rows(r, h):
        for b in range(blocks):
            column = jnp.sum(ra[h, b * LANES : (b + 1) * LANES, :], axis=1, keepdims=True)
            kab[r, h, 0, 0, b : b + 1, :] = to_lanes(column)

    def row_total(r, h):
        return sum(kab[r, h, n, 0] for n in range(8))

    def col_total(r, h, n):
        return sum(pbb[r, h, m, n] for m in range(16))

    loads[2].wait()
    loads[3].wait()
    for h in range(HEADS):
        output_product(h)
        arrive(pb_copies(0, h))
        logc = merge([(pbb[0, h, n, 0], pbb[0, h, n, 1]) for n in range(16)])
        logc = jnp.where(valid, logc, 0.0)
        kappa = jnp.where(valid, jnp.exp2(pbb[0, h, 0, 0] - logc), 0.0)
        cp[h, LOGC] = logc
        cp[h, KAPPA] = kappa
        spread_cols(kappa * jnp.exp2((1.0 - RELAX) * logc), RHO, h)
        spread_cols(kappa * jnp.exp2(logc), SIGMA, h)
        row_sums(RHO, 1, h)
        start(ka_copies(1, h))

    def second_columns(h):
        spread_rows(1.0 / row_total(1, h), rw, h)

        def body(g, accs):
            sl = group(g)
            kw = kk[h, sl, :] * wide(rw[h, sl, :])
            return accs[0] + kw, accs[1] + kw * dd[h, sl, :]

        zero = jnp.zeros((8, cols), F32)
        mass, adjoint = lax.fori_loop(0, groups, body, (zero, zero), unroll=4)
        kappa = cp[h, KAPPA]
        pack_cols(jnp.sum(mass, axis=0, keepdims=True), pbb.at[1, h, 0, 0])
        pack_cols(jnp.sum(adjoint, axis=0, keepdims=True), pbb.at[1, h, 0, 1])
        pbb[1, h, 0, 0] = pbb[1, h, 0, 0] * kappa
        pbb[1, h, 0, 1] = pbb[1, h, 0, 1] * kappa

    for h in range(HEADS):
        arrive(ka_copies(1, h))
        second_columns(h)
        start(pb_copies(1, h))
        qt[h] = q[:, head(h)].astype(F32).T.astype(BF16)
        ot[h] = o[:, head(h)].astype(F32).T.astype(BF16)

    def second_rows(h):
        mass = jnp.where(valid, col_total(1, h, 0), 1.0)
        kappa = cp[h, KAPPA]
        power = jnp.exp2((1.0 - RELAX) * cp[h, LOGC] - RELAX * log2(mass))
        spread_cols(kappa * power, PROB, h)
        spread_cols(RELAX * power * col_total(1, h, 1) * kappa / mass, BETA, h)

        def body(g, c):
            sl = group(g)
            t = (kk[h, sl, :] * wide(rw[h, sl, :])) * (dd[h, sl, :] * cv[h, PROB] - cv[h, BETA])
            dd[h, sl, :] = t
            ra[h, sl, :] = fold(t, jnp.add)
            return c

        lax.fori_loop(0, groups, body, 0, unroll=4)
        pack_rows(2, h)

    for h in range(HEADS):
        arrive(pb_copies(1, h))
        second_rows(h)
        start(ka_copies(2, h))

    HH = HD // 2

    def half(e):
        return slice(e * HH, (e + 1) * HH)

    def along(e, t):
        return ((z * 4 + t), ka) if e == 0 else ((t * 4 + y), ka)

    def rs_first(w, h, e, part):
        copies = []
        for a in HOPS:
            t = lax.rem((y if e == 0 else z) + a, 4)
            copies.append(
                pltpu.make_async_remote_copy(
                    src_ref=part.at[h, :, t, half(e)] if e == 0 else part.at[h, t, :, half(e)],
                    dst_ref=s1.at[w, h, e, a - 1],
                    send_sem=s1_s.at[w, h, e, a - 1], recv_sem=s1_r.at[w, h, e, a - 1],
                    device_id=along(e, t), device_id_type=MESH,
                )
            )
        return copies

    def rs_second(w, h, e):
        copies = []
        for a in HOPS:
            t = lax.rem((z if e == 0 else y) + a, 4)
            copies.append(
                pltpu.make_async_remote_copy(
                    src_ref=p1.at[w, h, e, t], dst_ref=s2.at[w, h, e, a - 1],
                    send_sem=s2_s.at[w, h, e, a - 1], recv_sem=s2_r.at[w, h, e, a - 1],
                    device_id=along(1 - e, t), device_id_type=MESH,
                )
            )
        return copies

    def rs_start(w, h, part):
        for e in range(2):
            start(rs_first(w, h, e, part))

    def rs_middle(w, h, part):
        for e in range(2):
            arrive(rs_first(w, h, e, part))
            for t in range(4):
                own = part[h, t, y, half(e)] if e == 0 else part[h, z, t, half(e)]
                p1[w, h, e, t] = (own + s1[w, h, e, 0, t]) + (s1[w, h, e, 1, t] + s1[w, h, e, 2, t])
            start(rs_second(w, h, e))

    def rs_last(w, h, scale, out):
        halves = []
        for e in range(2):
            arrive(rs_second(w, h, e))
            t = z if e == 0 else y
            halves.append((p1[w, h, e, t] + s2[w, h, e, 0]) + (s2[w, h, e, 1] + s2[w, h, e, 2]))
        out[:, head(h)] = jnp.concatenate(halves, axis=0).T * scale

    STRIP = 512

    def strips(body):
        for n in range(cols // STRIP):
            cs = slice(n * STRIP, (n + 1) * STRIP)
            lax.fori_loop(0, rows // 16, functools.partial(body, cs), 0, unroll=4)

    def strip_wide(column):
        return jnp.concatenate([column] * (STRIP // LANES), axis=1)

    def rows16(g):
        return pl.ds(pl.multiple_of(g * 16, 16), 16)

    def by_columns(lhs, part, h):
        res = jnp.dot(lhs[h], bb[...], preferred_element_type=F32)
        for t in range(tiles):
            part[h, t // 4, t % 4] = res[:, t * LANES : (t + 1) * LANES]

    def value_part(h):
        def body(cs, g, c):
            sl = rows16(g)
            prob = (kk[h, sl, cs] * strip_wide(rw[h, sl, :])) * cv[h, PROB, 0:1, cs]
            bb[sl, cs] = prob.astype(BF16)
            return c

        strips(body)
        by_columns(ot, dv, h)

    def first_adjoint(h):
        spread_rows(row_total(2, h), ry, h)

        def body(g, acc):
            sl = group(g)
            yw = ry[h, sl, :] * rw[h, sl, :]
            ry[h, sl, :] = yw
            return acc + kk[h, sl, :] * wide(yw)

        acc = lax.fori_loop(0, groups, body, jnp.zeros((8, cols), F32), unroll=8)
        pack_cols(jnp.sum(acc, axis=0, keepdims=True), pbb.at[2, h, 0, 0])
        pbb[2, h, 0, 0] = pbb[2, h, 0, 0] * cp[h, KAPPA]

    for h in range(HEADS):
        arrive(ka_copies(2, h))
        first_adjoint(h)
        start(pb_copies(2, h))
        if h == 0:
            value_part(0)
    rs_start(0, 0, dv)
    value_part(1)
    rs_start(0, 1, dv)

    for h in range(HEADS):
        arrive(pb_copies(2, h))
        adj = -jnp.exp2((1.0 - RELAX) * cp[h, LOGC]) * col_total(2, h, 0)
        spread_cols(RELAX * cp[h, KAPPA] * adj, GAMMA, h)
        row_sums(GAMMA, 3, h)
        start(ka_copies(3, h))

    def sq_copies(h):
        copies = []
        for n, off in enumerate(KA_OFFS):
            dev = ka_peer(off)
            copies.append(
                pltpu.make_async_remote_copy(
                    src_ref=dq.at[h, dev[1]], dst_ref=sq.at[h, n],
                    send_sem=sq_s.at[h, n], recv_sem=sq_r.at[h, n],
                    device_id=dev, device_id_type=MESH,
                )
            )
        return copies

    for h in range(HEADS):
        arrive(ka_copies(3, h))
        spread_rows(-row_total(3, h), ra, h)

        def body(cs, g, c):
            sl = rows16(g)
            low = strip_wide(ry[h, sl, :]) * cv[h, RHO, 0:1, cs] + cv[h, GAMMA, 0:1, cs]
            low = low + strip_wide(ra[h, sl, :]) * cv[h, SIGMA, 0:1, cs]
            bb[sl, cs] = (dd[h, sl, cs] - kk[h, sl, cs] * low).astype(BF16)
            return c

        strips(body)
        by_columns(qt, dk, h)
        rs_start(1, h, dk)
        res = jnp.dot(bb[...], k[:, head(h)], preferred_element_type=F32)
        for b in range(blocks):
            dq[h, b] = res[b * LANES : (b + 1) * LANES]
        start(sq_copies(h))
        rs_middle(0, h, dv)

    def query_last(h):
        arrive(sq_copies(h))
        total = dq[h, ka]
        for n in range(7):
            total = total + sq[h, n]
        gq_ref[:, head(h)] = total * HD**-0.5

    rs_middle(1, 0, dk)
    rs_last(0, 0, 1.0, gv_ref)
    query_last(0)
    rs_middle(1, 1, dk)
    rs_last(0, 1, 1.0, gv_ref)
    rs_last(1, 0, HD**-0.5, gk_ref)
    query_last(1)
    rs_last(1, 1, HD**-0.5, gk_ref)

    for h in range(HEADS):
        for r in range(4):
            drain(ka_copies(r, h))
        for r in range(3):
            drain(pb_copies(r, h))
        for w, part in ((0, dv), (1, dk)):
            for e in range(2):
                drain(rs_first(w, h, e, part))
                drain(rs_second(w, h, e))
        drain(sq_copies(h))


def settle(*refs):
    count = len(refs) // 2
    for n in range(count):
        refs[count + n][...] = refs[n][...]


def shards(queries, keys, values, grad_out, key_lengths):
    rows, width = queries.shape
    cols = keys.shape[0]
    vmem = lambda *shape: pltpu.VMEM(shape, F32)
    half = lambda *shape: pltpu.VMEM(shape, BF16)
    dma = lambda *shape: pltpu.SemaphoreType.DMA(shape)
    scratch = [
        half(rows, width), half(cols, width), half(cols, width), half(rows, width),
        half(HEADS, HD, rows), half(HEADS, HD, rows),
        vmem(HEADS, rows, cols), vmem(HEADS, rows, cols), half(rows, cols),
        vmem(HEADS, rows, LANES), vmem(HEADS, rows, LANES),
        vmem(HEADS, rows, LANES), vmem(HEADS, rows, LANES),
        vmem(HEADS, 6, 8, cols), vmem(HEADS, 2, cols // LANES, LANES),
        vmem(4, HEADS, 8, 2, rows // LANES, LANES),
        vmem(3, HEADS, 16, 2, cols // LANES, LANES),
        vmem(HEADS, 4, 4, HD, LANES), vmem(HEADS, 4, 4, HD, LANES),
        vmem(HEADS, rows // LANES, LANES, HD),
        vmem(2, HEADS, 2, 3, 4, HD // 2, LANES), vmem(2, HEADS, 2, 4, HD // 2, LANES),
        vmem(2, HEADS, 2, 3, HD // 2, LANES), vmem(HEADS, 7, LANES, HD),
        dma(4), dma(4, HEADS, 7), dma(4, HEADS, 7), dma(3, HEADS, 15), dma(3, HEADS, 15),
        dma(2, HEADS, 2, 3), dma(2, HEADS, 2, 3), dma(2, HEADS, 2, 3), dma(2, HEADS, 2, 3),
        dma(HEADS, 7), dma(HEADS, 7),
    ]
    hbm = pl.BlockSpec(memory_space=pl.ANY)
    here = pl.BlockSpec(memory_space=pltpu.VMEM)
    results = pl.pallas_call(
        functools.partial(kernel, rows, cols),
        out_shape=(
            jax.ShapeDtypeStruct((rows // 8, width), F32),
            jax.ShapeDtypeStruct((cols // 16, width), F32),
            jax.ShapeDtypeStruct((cols // 16, width), F32),
        ),
        in_specs=[pl.BlockSpec(memory_space=pltpu.SMEM), hbm, hbm, hbm, hbm],
        out_specs=(here, here, here),
        scratch_shapes=scratch,
        compiler_params=pltpu.CompilerParams(
            collective_id=0, has_side_effects=True, vmem_limit_bytes=60 * 2**20
        ),
        cost_estimate=pl.CostEstimate(
            flops=24 * rows * cols * HD, bytes_accessed=2**22, transcendentals=4 * rows * cols
        ),
    )(key_lengths, queries, keys, values, grad_out)
    return pl.pallas_call(
        settle,
        out_shape=tuple(jax.ShapeDtypeStruct(r.shape, F32) for r in results),
        in_specs=[here] * 3,
        out_specs=(here,) * 3,
    )(*results)


def solution(mesh):
    placed = (P("pb", None), P("ka", None), P("ka", None), P("pb", None), P("ka"))
    return jax.shard_map(
        shards,
        mesh=mesh,
        in_specs=placed,
        out_specs=(P(("pb", "ka"), None), P(("ka", "pb"), None), P(("ka", "pb"), None)),
        check_vma=False,
    )
```

```python
import functools

import jax
import jax.numpy as jnp
from jax import lax
from jax.experimental import pallas as pl
from jax.experimental.pallas import tpu as pltpu
from jax.sharding import PartitionSpec as P

HD = 128
HEADS = 2
LANES = 128
RELAX = 0.9
LOG2E = 1.4426950408889634
MESH = pl.DeviceIdType.MESH
F32 = jnp.float32
BF16 = jnp.bfloat16
NEG = -1e30


def far(n):
    return min(n, 4 - n)


KA_OFFS = sorted(
    [(a, c) for a in range(4) for c in range(2) if a or c], key=lambda o: -far(o[0])
)
PB_OFFS = sorted(
    [(a, b) for a in range(4) for b in range(4) if a or b], key=lambda o: -far(o[0]) - far(o[1])
)
HOPS = (2, 1, 3)


def kernel(
    rows, cols, len_ref, q_hbm, k_hbm, v_hbm, o_hbm, gq_ref, gk_ref, gv_ref,
    q, k, v, o, qt, ot, kk, dd, bb, ra, rb, rw, ry, cv, cp,
    kab, pbb, dv, dk, dq, s1, p1, s2, sq,
    in_sem, ka_s, ka_r, pb_s, pb_r, s1_s, s1_r, s2_s, s2_r, sq_s, sq_r,
):
    tiles = cols // LANES
    blocks = rows // LANES
    groups = rows // 8
    pb, ka = lax.axis_index("pb"), lax.axis_index("ka")
    z, y = pb // 4, lax.rem(pb, 4)
    xx, cc = ka // 2, lax.rem(ka, 2)

    def ka_peer(off):
        return (pb, lax.rem(xx + off[0], 4) * 2 + lax.rem(cc + off[1], 2))

    def pb_peer(off):
        return (lax.rem(z + off[0], 4) * 4 + lax.rem(y + off[1], 4), ka)

    ka_devs = [ka_peer(off) for off in KA_OFFS]
    pb_devs = [pb_peer(off) for off in PB_OFFS]

    loads = [
        pltpu.make_async_copy(src, dst, in_sem.at[n])
        for n, (src, dst) in enumerate(((q_hbm, q), (k_hbm, k), (v_hbm, v), (o_hbm, o)))
    ]
    for copy in loads:
        copy.start()
    barrier = pltpu.get_barrier_semaphore()
    for dev in pb_devs + ka_devs:
        pl.semaphore_signal(barrier, inc=1, device_id=dev, device_id_type=MESH)

    def ka_copies(r, h):
        return [
            pltpu.make_async_remote_copy(
                src_ref=kab.at[r, h, 0], dst_ref=kab.at[r, h, n + 1],
                send_sem=ka_s.at[r, h, n], recv_sem=ka_r.at[r, h, n],
                device_id=dev, device_id_type=MESH,
            )
            for n, dev in enumerate(ka_devs)
        ]

    def pb_copies(r, h):
        return [
            pltpu.make_async_remote_copy(
                src_ref=pbb.at[r, h, 0], dst_ref=pbb.at[r, h, n + 1],
                send_sem=pb_s.at[r, h, n], recv_sem=pb_r.at[r, h, n],
                device_id=dev, device_id_type=MESH,
            )
            for n, dev in enumerate(pb_devs)
        ]

    def start(copies):
        for copy in copies:
            copy.start()

    def arrive(copies):
        for copy in copies:
            copy.wait_recv()

    def each_head(step):
        def body(h, c):
            step(h)
            return c

        lax.fori_loop(0, HEADS, body, 0)

    def drain(copies):
        for copy in copies:
            copy.wait_send()

    eye = lax.broadcasted_iota(jnp.int32, (LANES, LANES), 0) == lax.broadcasted_iota(
        jnp.int32, (LANES, LANES), 1
    )
    position = lax.broadcasted_iota(jnp.int32, (tiles, LANES), 0) * LANES + lax.broadcasted_iota(
        jnp.int32, (tiles, LANES), 1
    )
    valid = position < len_ref[0]

    def to_lanes(column):
        return jnp.sum(jnp.where(eye, column, 0.0), axis=0, keepdims=True)

    def spread_rows(compact, ref, h):
        for b in range(blocks):
            column = jnp.sum(jnp.where(eye, compact[b : b + 1, :], 0.0), axis=1, keepdims=True)
            ref[h, b * LANES : (b + 1) * LANES, :] = jnp.broadcast_to(column, (LANES, LANES))

    def spread_cols(compact, n, h):
        for t in range(tiles):
            cv[h, n, :, t * LANES : (t + 1) * LANES] = jnp.broadcast_to(
                compact[t : t + 1, :], (8, LANES)
            )

    def pack_cols(line, ref):
        for t in range(tiles):
            ref[t : t + 1, :] = line[:, t * LANES : (t + 1) * LANES]

    def wide(column):
        return jnp.concatenate([column] * tiles, axis=1)

    def fold(block, op):
        parts = [block[:, t * LANES : (t + 1) * LANES] for t in range(tiles)]
        while len(parts) > 1:
            parts = [op(a, b) for a, b in zip(parts[::2], parts[1::2])]
        return parts[0]

    def group(g):
        return pl.ds(pl.multiple_of(g * 8, 8), 8)

    def log2(x):
        return jnp.log(x) * LOG2E

    BIAS, RHO, PROB, BETA, GAMMA, SIGMA = range(6)
    LOGC, KAPPA = range(2)
    spread_cols(jnp.where(valid, 0.0, NEG), BIAS, 0)

    def head(h):
        return pl.ds(h * HD if isinstance(h, int) else pl.multiple_of(h * HD, HD), HD)

    def product(a, b, h):
        return lax.dot_general(
            a[:, head(h)], b[:, head(h)], (((1,), (1,)), ((), ())), preferred_element_type=F32
        )

    def scores(h):
        kk[h] = product(q, k, h) * (HD**-0.5 * LOG2E) + cv[0, BIAS, 0:1, :]

        def sweep(g, c):
            sl = group(g)
            s = kk[h, sl, :]
            peak = fold(s, jnp.maximum)
            ra[h, sl, :] = peak
            rb[h, sl, :] = fold(jnp.exp2(s - wide(peak)), jnp.add)
            return c

        lax.fori_loop(0, groups, sweep, 0, unroll=16)
        for b in range(blocks):
            sl = slice(b * LANES, (b + 1) * LANES)
            peak = ra[h, sl, :]
            highest = jnp.max(peak, axis=1, keepdims=True)
            mass = jnp.sum(rb[h, sl, :] * jnp.exp2(peak - highest), axis=1, keepdims=True)
            kab[0, h, 0, 0, b : b + 1, :] = to_lanes(highest)
            kab[0, h, 0, 1, b : b + 1, :] = to_lanes(mass)

    loads[0].wait()
    loads[1].wait()
    scores(0)
    pl.semaphore_wait(barrier, len(KA_OFFS) + len(PB_OFFS))
    start(ka_copies(0, 0))
    scores(1)
    start(ka_copies(0, 1))

    def output_product(h):
        dd[h] = product(o, v, h)

    def merge(parts):
        highest = parts[0][0]
        for m, _ in parts[1:]:
            highest = jnp.maximum(highest, m)
        mass = sum(s * jnp.exp2(m - highest) for m, s in parts)
        return highest + log2(mass)

    def first_columns(h):
        pot = -merge([(kab[0, h, n, 0], kab[0, h, n, 1]) for n in range(8)])
        spread_rows(pot, rw, h)

        def peaks(g, acc):
            sl = group(g)
            return jnp.maximum(acc, kk[h, sl, :] + wide(rw[h, sl, :]))

        acc = lax.fori_loop(0, groups, peaks, jnp.full((8, cols), NEG, F32), unroll=8)
        peak = jnp.maximum(jnp.max(acc, axis=0, keepdims=True), -1e4)
        cv[h, PROB] = jnp.broadcast_to(peak, (8, cols))

        def masses(g, acc):
            sl = pl.ds(pl.multiple_of(g * 32, 32), 32)
            pot = rw[h, sl, :]
            out = []
            for t in range(tiles):
                cs = slice(t * LANES, (t + 1) * LANES)
                e = jnp.exp2(kk[h, sl, cs] + pot - cv[h, PROB, 0:1, cs])
                kk[h, sl, cs] = e
                out.append(acc[:, cs] + ((e[:8] + e[8:16]) + (e[16:24] + e[24:])))
            return jnp.concatenate(out, axis=1)

        acc = lax.fori_loop(0, rows // 32, masses, jnp.zeros((8, cols), F32))
        pack_cols(peak, pbb.at[0, h, 0, 0])
        pack_cols(jnp.sum(acc, axis=0, keepdims=True), pbb.at[0, h, 0, 1])

    @each_head
    def _(h):
        arrive(ka_copies(0, h))
        first_columns(h)
        start(pb_copies(0, h))

    def row_sums(n, r, h):
        x = cv[h, n]

        def body(g, c):
            sl = group(g)
            ra[h, sl, :] = fold(kk[h, sl, :] * x, jnp.add)
            return c

        lax.fori_loop(0, groups, body, 0, unroll=8)
        pack_rows(r, h)

    def pack_rows(r, h):
        for b in range(blocks):
            column = jnp.sum(ra[h, b * LANES : (b + 1) * LANES, :], axis=1, keepdims=True)
            kab[r, h, 0, 0, b : b + 1, :] = to_lanes(column)

    def row_total(r, h):
        return sum(kab[r, h, n, 0] for n in range(8))

    def col_total(r, h, n):
        return sum(pbb[r, h, m, n] for m in range(16))

    loads[2].wait()
    loads[3].wait()
    @each_head
    def _(h):
        output_product(h)
        arrive(pb_copies(0, h))
        logc = merge([(pbb[0, h, n, 0], pbb[0, h, n, 1]) for n in range(16)])
        logc = jnp.where(valid, logc, 0.0)
        kappa = jnp.where(valid, jnp.exp2(pbb[0, h, 0, 0] - logc), 0.0)
        cp[h, LOGC] = logc
        cp[h, KAPPA] = kappa
        spread_cols(kappa * jnp.exp2((1.0 - RELAX) * logc), RHO, h)
        spread_cols(kappa * jnp.exp2(logc), SIGMA, h)
        row_sums(RHO, 1, h)
        start(ka_copies(1, h))

    def second_columns(h):
        spread_rows(1.0 / row_total(1, h), rw, h)

        def body(g, accs):
            sl = group(g)
            kw = kk[h, sl, :] * wide(rw[h, sl, :])
            return accs[0] + kw, accs[1] + kw * dd[h, sl, :]

        zero = jnp.zeros((8, cols), F32)
        mass, adjoint = lax.fori_loop(0, groups, body, (zero, zero), unroll=4)
        kappa = cp[h, KAPPA]
        pack_cols(jnp.sum(mass, axis=0, keepdims=True), pbb.at[1, h, 0, 0])
        pack_cols(jnp.sum(adjoint, axis=0, keepdims=True), pbb.at[1, h, 0, 1])
        pbb[1, h, 0, 0] = pbb[1, h, 0, 0] * kappa
        pbb[1, h, 0, 1] = pbb[1, h, 0, 1] * kappa

    @each_head
    def _(h):
        arrive(ka_copies(1, h))
        second_columns(h)
        start(pb_copies(1, h))
        qt[h] = q[:, head(h)].astype(F32).T.astype(BF16)
        ot[h] = o[:, head(h)].astype(F32).T.astype(BF16)

    def second_rows(h):
        mass = jnp.where(valid, col_total(1, h, 0), 1.0)
        kappa = cp[h, KAPPA]
        power = jnp.exp2((1.0 - RELAX) * cp[h, LOGC] - RELAX * log2(mass))
        spread_cols(kappa * power, PROB, h)
        spread_cols(RELAX * power * col_total(1, h, 1) * kappa / mass, BETA, h)

        def body(g, c):
            sl = group(g)
            t = (kk[h, sl, :] * wide(rw[h, sl, :])) * (dd[h, sl, :] * cv[h, PROB] - cv[h, BETA])
            dd[h, sl, :] = t
            ra[h, sl, :] = fold(t, jnp.add)
            return c

        lax.fori_loop(0, groups, body, 0, unroll=4)
        pack_rows(2, h)

    @each_head
    def _(h):
        arrive(pb_copies(1, h))
        second_rows(h)
        start(ka_copies(2, h))

    HH = HD // 2

    def half(e):
        return slice(e * HH, (e + 1) * HH)

    def along(e, t):
        return ((z * 4 + t), ka) if e == 0 else ((t * 4 + y), ka)

    def rs_first(w, h, e, part):
        copies = []
        for a in HOPS:
            t = lax.rem((y if e == 0 else z) + a, 4)
            copies.append(
                pltpu.make_async_remote_copy(
                    src_ref=part.at[h, :, t, half(e)] if e == 0 else part.at[h, t, :, half(e)],
                    dst_ref=s1.at[w, h, e, a - 1],
                    send_sem=s1_s.at[w, h, e, a - 1], recv_sem=s1_r.at[w, h, e, a - 1],
                    device_id=along(e, t), device_id_type=MESH,
                )
            )
        return copies

    def rs_second(w, h, e):
        copies = []
        for a in HOPS:
            t = lax.rem((z if e == 0 else y) + a, 4)
            copies.append(
                pltpu.make_async_remote_copy(
                    src_ref=p1.at[w, h, e, t], dst_ref=s2.at[w, h, e, a - 1],
                    send_sem=s2_s.at[w, h, e, a - 1], recv_sem=s2_r.at[w, h, e, a - 1],
                    device_id=along(1 - e, t), device_id_type=MESH,
                )
            )
        return copies

    def rs_start(w, h, part):
        for e in range(2):
            start(rs_first(w, h, e, part))

    def rs_middle(w, h, part):
        for e in range(2):
            arrive(rs_first(w, h, e, part))
            for t in range(4):
                own = part[h, t, y, half(e)] if e == 0 else part[h, z, t, half(e)]
                p1[w, h, e, t] = (own + s1[w, h, e, 0, t]) + (s1[w, h, e, 1, t] + s1[w, h, e, 2, t])
            start(rs_second(w, h, e))

    def rs_last(w, h, scale, out):
        halves = []
        for e in range(2):
            arrive(rs_second(w, h, e))
            t = z if e == 0 else y
            halves.append((p1[w, h, e, t] + s2[w, h, e, 0]) + (s2[w, h, e, 1] + s2[w, h, e, 2]))
        out[:, head(h)] = jnp.concatenate(halves, axis=0).T * scale

    STRIP = 512

    def strips(body):
        for n in range(cols // STRIP):
            cs = slice(n * STRIP, (n + 1) * STRIP)
            lax.fori_loop(0, rows // 16, functools.partial(body, cs), 0, unroll=4)

    def strip_wide(column):
        return jnp.concatenate([column] * (STRIP // LANES), axis=1)

    def rows16(g):
        return pl.ds(pl.multiple_of(g * 16, 16), 16)

    def by_columns(lhs, part, h):
        res = jnp.dot(lhs[h], bb[...], preferred_element_type=F32)
        for t in range(tiles):
            part[h, t // 4, t % 4] = res[:, t * LANES : (t + 1) * LANES]

    def value_part(h):
        def body(cs, g, c):
            sl = rows16(g)
            prob = (kk[h, sl, cs] * strip_wide(rw[h, sl, :])) * cv[h, PROB, 0:1, cs]
            bb[sl, cs] = prob.astype(BF16)
            return c

        strips(body)
        by_columns(ot, dv, h)

    def first_adjoint(h):
        spread_rows(row_total(2, h), ry, h)

        def body(g, acc):
            sl = group(g)
            yw = ry[h, sl, :] * rw[h, sl, :]
            ry[h, sl, :] = yw
            return acc + kk[h, sl, :] * wide(yw)

        acc = lax.fori_loop(0, groups, body, jnp.zeros((8, cols), F32), unroll=8)
        pack_cols(jnp.sum(acc, axis=0, keepdims=True), pbb.at[2, h, 0, 0])
        pbb[2, h, 0, 0] = pbb[2, h, 0, 0] * cp[h, KAPPA]

    for h in range(HEADS):
        arrive(ka_copies(2, h))
        first_adjoint(h)
        start(pb_copies(2, h))
        if h == 0:
            value_part(0)
    rs_start(0, 0, dv)
    value_part(1)
    rs_start(0, 1, dv)

    @each_head
    def _(h):
        arrive(pb_copies(2, h))
        adj = -jnp.exp2((1.0 - RELAX) * cp[h, LOGC]) * col_total(2, h, 0)
        spread_cols(RELAX * cp[h, KAPPA] * adj, GAMMA, h)
        row_sums(GAMMA, 3, h)
        start(ka_copies(3, h))

    def sq_copies(h):
        copies = []
        for n, dev in enumerate(ka_devs):
            copies.append(
                pltpu.make_async_remote_copy(
                    src_ref=dq.at[h, dev[1]], dst_ref=sq.at[h, n],
                    send_sem=sq_s.at[h, n], recv_sem=sq_r.at[h, n],
                    device_id=dev, device_id_type=MESH,
                )
            )
        return copies

    @each_head
    def _(h):
        arrive(ka_copies(3, h))
        spread_rows(-row_total(3, h), ra, h)

        def body(cs, g, c):
            sl = rows16(g)
            low = strip_wide(ry[h, sl, :]) * cv[h, RHO, 0:1, cs] + cv[h, GAMMA, 0:1, cs]
            low = low + strip_wide(ra[h, sl, :]) * cv[h, SIGMA, 0:1, cs]
            bb[sl, cs] = (dd[h, sl, cs] - kk[h, sl, cs] * low).astype(BF16)
            return c

        strips(body)
        by_columns(qt, dk, h)
        rs_start(1, h, dk)
        res = jnp.dot(bb[...], k[:, head(h)], preferred_element_type=F32)
        for b in range(blocks):
            dq[h, b] = res[b * LANES : (b + 1) * LANES]
        start(sq_copies(h))

    def query_last(h):
        arrive(sq_copies(h))
        total = dq[h, ka]
        for n in range(7):
            total = total + sq[h, n]
        gq_ref[:, head(h)] = total * HD**-0.5

    rs_middle(0, 0, dv)
    rs_middle(0, 1, dv)
    rs_middle(1, 0, dk)
    rs_last(0, 0, 1.0, gv_ref)
    query_last(0)
    for h in range(HEADS):
        for r in range(4):
            drain(ka_copies(r, h))
        for r in range(3):
            drain(pb_copies(r, h))
        for e in range(2):
            drain(rs_first(0, h, e, dv))
        drain(sq_copies(h))
    for e in range(2):
        drain(rs_first(1, 0, e, dk))
    rs_middle(1, 1, dk)
    for e in range(2):
        drain(rs_first(1, 1, e, dk))
    rs_last(0, 1, 1.0, gv_ref)
    rs_last(1, 0, HD**-0.5, gk_ref)
    query_last(1)
    rs_last(1, 1, HD**-0.5, gk_ref)

    for h in range(HEADS):
        for w in range(2):
            for e in range(2):
                drain(rs_second(w, h, e))


def settle(*refs):
    count = len(refs) // 2
    for n in range(count):
        refs[count + n][...] = refs[n][...]


def shards(queries, keys, values, grad_out, key_lengths):
    rows, width = queries.shape
    cols = keys.shape[0]
    vmem = lambda *shape: pltpu.VMEM(shape, F32)
    half = lambda *shape: pltpu.VMEM(shape, BF16)
    dma = lambda *shape: pltpu.SemaphoreType.DMA(shape)
    scratch = [
        half(rows, width), half(cols, width), half(cols, width), half(rows, width),
        half(HEADS, HD, rows), half(HEADS, HD, rows),
        vmem(HEADS, rows, cols), vmem(HEADS, rows, cols), half(rows, cols),
        vmem(HEADS, rows, LANES), vmem(HEADS, rows, LANES),
        vmem(HEADS, rows, LANES), vmem(HEADS, rows, LANES),
        vmem(HEADS, 6, 8, cols), vmem(HEADS, 2, cols // LANES, LANES),
        vmem(4, HEADS, 8, 2, rows // LANES, LANES),
        vmem(3, HEADS, 16, 2, cols // LANES, LANES),
        vmem(HEADS, 4, 4, HD, LANES), vmem(HEADS, 4, 4, HD, LANES),
        vmem(HEADS, rows // LANES, LANES, HD),
        vmem(2, HEADS, 2, 3, 4, HD // 2, LANES), vmem(2, HEADS, 2, 4, HD // 2, LANES),
        vmem(2, HEADS, 2, 3, HD // 2, LANES), vmem(HEADS, 7, LANES, HD),
        dma(4), dma(4, HEADS, 7), dma(4, HEADS, 7), dma(3, HEADS, 15), dma(3, HEADS, 15),
        dma(2, HEADS, 2, 3), dma(2, HEADS, 2, 3), dma(2, HEADS, 2, 3), dma(2, HEADS, 2, 3),
        dma(HEADS, 7), dma(HEADS, 7),
    ]
    hbm = pl.BlockSpec(memory_space=pl.ANY)
    here = pl.BlockSpec(memory_space=pltpu.VMEM)
    results = pl.pallas_call(
        functools.partial(kernel, rows, cols),
        out_shape=(
            jax.ShapeDtypeStruct((rows // 8, width), F32),
            jax.ShapeDtypeStruct((cols // 16, width), F32),
            jax.ShapeDtypeStruct((cols // 16, width), F32),
        ),
        in_specs=[pl.BlockSpec(memory_space=pltpu.SMEM), hbm, hbm, hbm, hbm],
        out_specs=(here, here, here),
        scratch_shapes=scratch,
        compiler_params=pltpu.CompilerParams(
            collective_id=0, has_side_effects=True, vmem_limit_bytes=60 * 2**20
        ),
        cost_estimate=pl.CostEstimate(
            flops=24 * rows * cols * HD, bytes_accessed=2**22, transcendentals=4 * rows * cols
        ),
    )(key_lengths, queries, keys, values, grad_out)
    return pl.pallas_call(
        settle,
        out_shape=tuple(jax.ShapeDtypeStruct(r.shape, F32) for r in results),
        in_specs=[here] * 3,
        out_specs=(here,) * 3,
    )(*results)


def solution(mesh):
    placed = (P("pb", None), P("ka", None), P("ka", None), P("pb", None), P("ka"))
    return jax.shard_map(
        shards,
        mesh=mesh,
        in_specs=placed,
        out_specs=(P(("pb", "ka"), None), P(("ka", "pb"), None), P(("ka", "pb"), None)),
        check_vma=False,
    )
```

```python
import functools

import jax
import jax.numpy as jnp
from jax import lax
from jax.experimental import pallas as pl
from jax.experimental.pallas import tpu as pltpu
from jax.sharding import PartitionSpec as P

HD = 128
HEADS = 2
LANES = 128
RELAX = 0.9
LOG2E = 1.4426950408889634
MESH = pl.DeviceIdType.MESH
F32 = jnp.float32
BF16 = jnp.bfloat16
NEG = -1e30


def far(n):
    return min(n, 4 - n)


KA_OFFS = sorted(
    [(a, c) for a in range(4) for c in range(2) if a or c], key=lambda o: -far(o[0])
)
PB_OFFS = sorted(
    [(a, b) for a in range(4) for b in range(4) if a or b], key=lambda o: -far(o[0]) - far(o[1])
)
HOPS = (2, 1, 3)


def kernel(
    rows, cols, len_ref, q_hbm, k_hbm, v_hbm, o_hbm, gq_ref, gk_ref, gv_ref,
    q, k, v, o, qt, ot, kk, dd, bb, ra, rb, rw, ry, cv, cp,
    kab, pbb, dv, dk, dq, s1, p1, s2, sq,
    in_sem, ka_s, ka_r, pb_s, pb_r, s1_s, s1_r, s2_s, s2_r, sq_s, sq_r,
):
    tiles = cols // LANES
    blocks = rows // LANES
    groups = rows // 8
    pb, ka = lax.axis_index("pb"), lax.axis_index("ka")
    z, y = pb // 4, lax.rem(pb, 4)
    xx, cc = ka // 2, lax.rem(ka, 2)

    def ka_peer(off):
        return (pb, lax.rem(xx + off[0], 4) * 2 + lax.rem(cc + off[1], 2))

    def pb_peer(off):
        return (lax.rem(z + off[0], 4) * 4 + lax.rem(y + off[1], 4), ka)

    ka_devs = [ka_peer(off) for off in KA_OFFS]
    pb_devs = [pb_peer(off) for off in PB_OFFS]

    loads = [
        pltpu.make_async_copy(src, dst, in_sem.at[n])
        for n, (src, dst) in enumerate(((q_hbm, q), (k_hbm, k), (v_hbm, v), (o_hbm, o)))
    ]
    for copy in loads:
        copy.start()
    barrier = pltpu.get_barrier_semaphore()
    for dev in pb_devs + ka_devs:
        pl.semaphore_signal(barrier, inc=1, device_id=dev, device_id_type=MESH)

    def ka_copies(r, h):
        return [
            pltpu.make_async_remote_copy(
                src_ref=kab.at[r, h, 0], dst_ref=kab.at[r, h, n + 1],
                send_sem=ka_s.at[r, h, n], recv_sem=ka_r.at[r, h, n],
                device_id=dev, device_id_type=MESH,
            )
            for n, dev in enumerate(ka_devs)
        ]

    def pb_copies(r, h):
        return [
            pltpu.make_async_remote_copy(
                src_ref=pbb.at[r, h, 0], dst_ref=pbb.at[r, h, n + 1],
                send_sem=pb_s.at[r, h, n], recv_sem=pb_r.at[r, h, n],
                device_id=dev, device_id_type=MESH,
            )
            for n, dev in enumerate(pb_devs)
        ]

    def start(copies):
        for copy in copies:
            copy.start()

    def arrive(copies):
        for copy in copies:
            copy.wait_recv()

    def each_head(step):
        def body(h, c):
            step(h)
            return c

        lax.fori_loop(0, HEADS, body, 0)

    def drain(copies):
        for copy in copies:
            copy.wait_send()

    eye = lax.broadcasted_iota(jnp.int32, (LANES, LANES), 0) == lax.broadcasted_iota(
        jnp.int32, (LANES, LANES), 1
    )
    position = lax.broadcasted_iota(jnp.int32, (tiles, LANES), 0) * LANES + lax.broadcasted_iota(
        jnp.int32, (tiles, LANES), 1
    )
    valid = position < len_ref[0]

    def to_lanes(column):
        return jnp.sum(jnp.where(eye, column, 0.0), axis=0, keepdims=True)

    def spread_rows(compact, ref, h):
        for b in range(blocks):
            column = jnp.sum(jnp.where(eye, compact[b : b + 1, :], 0.0), axis=1, keepdims=True)
            ref[h, b * LANES : (b + 1) * LANES, :] = jnp.broadcast_to(column, (LANES, LANES))

    def spread_cols(compact, n, h):
        for t in range(tiles):
            cv[h, n, :, t * LANES : (t + 1) * LANES] = jnp.broadcast_to(
                compact[t : t + 1, :], (8, LANES)
            )

    def pack_cols(line, ref):
        for t in range(tiles):
            ref[t : t + 1, :] = line[:, t * LANES : (t + 1) * LANES]

    def wide(column):
        return jnp.concatenate([column] * tiles, axis=1)

    def fold(block, op):
        parts = [block[:, t * LANES : (t + 1) * LANES] for t in range(tiles)]
        while len(parts) > 1:
            parts = [op(a, b) for a, b in zip(parts[::2], parts[1::2])]
        return parts[0]

    def group(g):
        return pl.ds(pl.multiple_of(g * 8, 8), 8)

    def log2(x):
        return jnp.log(x) * LOG2E

    BIAS, RHO, PROB, BETA, GAMMA, SIGMA = range(6)
    LOGC, KAPPA = range(2)
    spread_cols(jnp.where(valid, 0.0, NEG), BIAS, 0)

    def head(h):
        return pl.ds(h * HD if isinstance(h, int) else pl.multiple_of(h * HD, HD), HD)

    def product(a, b, h):
        return lax.dot_general(
            a[:, head(h)], b[:, head(h)], (((1,), (1,)), ((), ())), preferred_element_type=F32
        )

    def scores(h):
        kk[h] = product(q, k, h) * (HD**-0.5 * LOG2E) + cv[0, BIAS, 0:1, :]

        def sweep(g, c):
            sl = group(g)
            s = kk[h, sl, :]
            peak = fold(s, jnp.maximum)
            ra[h, sl, :] = peak
            rb[h, sl, :] = fold(jnp.exp2(s - wide(peak)), jnp.add)
            return c

        lax.fori_loop(0, groups, sweep, 0, unroll=16)
        for b in range(blocks):
            sl = slice(b * LANES, (b + 1) * LANES)
            peak = ra[h, sl, :]
            highest = jnp.max(peak, axis=1, keepdims=True)
            mass = jnp.sum(rb[h, sl, :] * jnp.exp2(peak - highest), axis=1, keepdims=True)
            kab[0, h, 0, 0, b : b + 1, :] = to_lanes(highest)
            kab[0, h, 0, 1, b : b + 1, :] = to_lanes(mass)

    loads[0].wait()
    loads[1].wait()
    scores(0)
    pl.semaphore_wait(barrier, len(KA_OFFS) + len(PB_OFFS))
    start(ka_copies(0, 0))
    scores(1)
    start(ka_copies(0, 1))

    def output_product(h):
        dd[h] = product(o, v, h)

    def merge(parts):
        highest = parts[0][0]
        for m, _ in parts[1:]:
            highest = jnp.maximum(highest, m)
        mass = sum(s * jnp.exp2(m - highest) for m, s in parts)
        return highest + log2(mass)

    def first_columns(h):
        pot = -merge([(kab[0, h, n, 0], kab[0, h, n, 1]) for n in range(8)])
        spread_rows(pot, rw, h)

        def peaks(g, acc):
            sl = group(g)
            return jnp.maximum(acc, kk[h, sl, :] + wide(rw[h, sl, :]))

        acc = lax.fori_loop(0, groups, peaks, jnp.full((8, cols), NEG, F32), unroll=8)
        peak = jnp.maximum(jnp.max(acc, axis=0, keepdims=True), -1e4)
        cv[h, PROB] = jnp.broadcast_to(peak, (8, cols))

        def masses(g, acc):
            sl = pl.ds(pl.multiple_of(g * 32, 32), 32)
            pot = rw[h, sl, :]
            out = []
            for t in range(tiles):
                cs = slice(t * LANES, (t + 1) * LANES)
                e = jnp.exp2(kk[h, sl, cs] + pot - cv[h, PROB, 0:1, cs])
                kk[h, sl, cs] = e
                out.append(acc[:, cs] + ((e[:8] + e[8:16]) + (e[16:24] + e[24:])))
            return jnp.concatenate(out, axis=1)

        acc = lax.fori_loop(0, rows // 32, masses, jnp.zeros((8, cols), F32))
        pack_cols(peak, pbb.at[0, h, 0, 0])
        pack_cols(jnp.sum(acc, axis=0, keepdims=True), pbb.at[0, h, 0, 1])

    @each_head
    def _(h):
        arrive(ka_copies(0, h))
        first_columns(h)
        start(pb_copies(0, h))

    def row_sums(n, r, h):
        x = cv[h, n]

        def body(g, c):
            sl = group(g)
            ra[h, sl, :] = fold(kk[h, sl, :] * x, jnp.add)
            return c

        lax.fori_loop(0, groups, body, 0, unroll=8)
        pack_rows(r, h)

    def pack_rows(r, h):
        for b in range(blocks):
            column = jnp.sum(ra[h, b * LANES : (b + 1) * LANES, :], axis=1, keepdims=True)
            kab[r, h, 0, 0, b : b + 1, :] = to_lanes(column)

    def row_total(r, h):
        return sum(kab[r, h, n, 0] for n in range(8))

    def col_total(r, h, n):
        return sum(pbb[r, h, m, n] for m in range(16))

    loads[2].wait()
    loads[3].wait()
    @each_head
    def _(h):
        output_product(h)
        arrive(pb_copies(0, h))
        logc = merge([(pbb[0, h, n, 0], pbb[0, h, n, 1]) for n in range(16)])
        logc = jnp.where(valid, logc, 0.0)
        kappa = jnp.where(valid, jnp.exp2(pbb[0, h, 0, 0] - logc), 0.0)
        cp[h, LOGC] = logc
        cp[h, KAPPA] = kappa
        spread_cols(kappa * jnp.exp2((1.0 - RELAX) * logc), RHO, h)
        spread_cols(kappa * jnp.exp2(logc), SIGMA, h)
        row_sums(RHO, 1, h)
        start(ka_copies(1, h))

    def second_columns(h):
        spread_rows(1.0 / row_total(1, h), rw, h)

        def body(g, accs):
            sl = group(g)
            kw = kk[h, sl, :] * wide(rw[h, sl, :])
            return accs[0] + kw, accs[1] + kw * dd[h, sl, :]

        zero = jnp.zeros((8, cols), F32)
        mass, adjoint = lax.fori_loop(0, groups, body, (zero, zero), unroll=4)
        kappa = cp[h, KAPPA]
        pack_cols(jnp.sum(mass, axis=0, keepdims=True), pbb.at[1, h, 0, 0])
        pack_cols(jnp.sum(adjoint, axis=0, keepdims=True), pbb.at[1, h, 0, 1])
        pbb[1, h, 0, 0] = pbb[1, h, 0, 0] * kappa
        pbb[1, h, 0, 1] = pbb[1, h, 0, 1] * kappa

    @each_head
    def _(h):
        arrive(ka_copies(1, h))
        second_columns(h)
        start(pb_copies(1, h))
        qt[h] = q[:, head(h)].astype(F32).T.astype(BF16)
        ot[h] = o[:, head(h)].astype(F32).T.astype(BF16)

    def second_rows(h):
        mass = jnp.where(valid, col_total(1, h, 0), 1.0)
        kappa = cp[h, KAPPA]
        power = jnp.exp2((1.0 - RELAX) * cp[h, LOGC] - RELAX * log2(mass))
        spread_cols(kappa * power, PROB, h)
        spread_cols(RELAX * power * col_total(1, h, 1) * kappa / mass, BETA, h)

        def body(g, c):
            sl = group(g)
            t = (kk[h, sl, :] * wide(rw[h, sl, :])) * (dd[h, sl, :] * cv[h, PROB] - cv[h, BETA])
            dd[h, sl, :] = t
            ra[h, sl, :] = fold(t, jnp.add)
            return c

        lax.fori_loop(0, groups, body, 0, unroll=4)
        pack_rows(2, h)

    @each_head
    def _(h):
        arrive(pb_copies(1, h))
        second_rows(h)
        start(ka_copies(2, h))

    HH = HD // 2

    def half(e):
        return slice(e * HH, (e + 1) * HH)

    def along(e, t):
        return ((z * 4 + t), ka) if e == 0 else ((t * 4 + y), ka)

    def rs_first(w, h, e, part):
        copies = []
        for a in HOPS:
            t = lax.rem((y if e == 0 else z) + a, 4)
            copies.append(
                pltpu.make_async_remote_copy(
                    src_ref=part.at[h, :, t, half(e)] if e == 0 else part.at[h, t, :, half(e)],
                    dst_ref=s1.at[w, h, e, a - 1],
                    send_sem=s1_s.at[w, h, e, a - 1], recv_sem=s1_r.at[w, h, e, a - 1],
                    device_id=along(e, t), device_id_type=MESH,
                )
            )
        return copies

    def rs_second(w, h, e):
        copies = []
        for a in HOPS:
            t = lax.rem((z if e == 0 else y) + a, 4)
            copies.append(
                pltpu.make_async_remote_copy(
                    src_ref=p1.at[w, h, e, t], dst_ref=s2.at[w, h, e, a - 1],
                    send_sem=s2_s.at[w, h, e, a - 1], recv_sem=s2_r.at[w, h, e, a - 1],
                    device_id=along(1 - e, t), device_id_type=MESH,
                )
            )
        return copies

    def rs_start(w, h, part):
        halves = [rs_first(w, h, e, part) for e in range(2)]
        for pair in zip(*halves):
            start(pair)

    def rs_middle(w, h, part):
        for e in range(2):
            arrive(rs_first(w, h, e, part))
            for t in range(4):
                own = part[h, t, y, half(e)] if e == 0 else part[h, z, t, half(e)]
                p1[w, h, e, t] = (own + s1[w, h, e, 0, t]) + (s1[w, h, e, 1, t] + s1[w, h, e, 2, t])
            start(rs_second(w, h, e))

    def rs_last(w, h, scale, out):
        halves = []
        for e in range(2):
            arrive(rs_second(w, h, e))
            t = z if e == 0 else y
            halves.append((p1[w, h, e, t] + s2[w, h, e, 0]) + (s2[w, h, e, 1] + s2[w, h, e, 2]))
        out[:, head(h)] = jnp.concatenate(halves, axis=0).T * scale

    STRIP = 512

    def strips(body):
        for n in range(cols // STRIP):
            cs = slice(n * STRIP, (n + 1) * STRIP)
            lax.fori_loop(0, rows // 16, functools.partial(body, cs), 0, unroll=4)

    def strip_wide(column):
        return jnp.concatenate([column] * (STRIP // LANES), axis=1)

    def rows16(g):
        return pl.ds(pl.multiple_of(g * 16, 16), 16)

    def by_columns(lhs, part, h):
        res = jnp.dot(lhs[h], bb[...], preferred_element_type=F32)
        for t in range(tiles):
            part[h, t // 4, t % 4] = res[:, t * LANES : (t + 1) * LANES]

    def value_part(h):
        def body(cs, g, c):
            sl = rows16(g)
            prob = (kk[h, sl, cs] * strip_wide(rw[h, sl, :])) * cv[h, PROB, 0:1, cs]
            bb[sl, cs] = prob.astype(BF16)
            return c

        strips(body)
        by_columns(ot, dv, h)

    def first_adjoint(h):
        spread_rows(row_total(2, h), ry, h)

        def body(g, acc):
            sl = group(g)
            yw = ry[h, sl, :] * rw[h, sl, :]
            ry[h, sl, :] = yw
            return acc + kk[h, sl, :] * wide(yw)

        acc = lax.fori_loop(0, groups, body, jnp.zeros((8, cols), F32), unroll=8)
        pack_cols(jnp.sum(acc, axis=0, keepdims=True), pbb.at[2, h, 0, 0])
        pbb[2, h, 0, 0] = pbb[2, h, 0, 0] * cp[h, KAPPA]

    for h in range(HEADS):
        arrive(ka_copies(2, h))
        first_adjoint(h)
        start(pb_copies(2, h))
        if h == 0:
            value_part(0)
    rs_start(0, 0, dv)
    value_part(1)
    rs_start(0, 1, dv)

    @each_head
    def _(h):
        arrive(pb_copies(2, h))
        adj = -jnp.exp2((1.0 - RELAX) * cp[h, LOGC]) * col_total(2, h, 0)
        spread_cols(RELAX * cp[h, KAPPA] * adj, GAMMA, h)
        row_sums(GAMMA, 3, h)
        start(ka_copies(3, h))

    def sq_copies(h):
        copies = []
        for n, dev in enumerate(ka_devs):
            copies.append(
                pltpu.make_async_remote_copy(
                    src_ref=dq.at[h, dev[1]], dst_ref=sq.at[h, n],
                    send_sem=sq_s.at[h, n], recv_sem=sq_r.at[h, n],
                    device_id=dev, device_id_type=MESH,
                )
            )
        return copies

    @each_head
    def _(h):
        arrive(ka_copies(3, h))
        spread_rows(-row_total(3, h), ra, h)

        def body(cs, g, c):
            sl = rows16(g)
            low = strip_wide(ry[h, sl, :]) * cv[h, RHO, 0:1, cs] + cv[h, GAMMA, 0:1, cs]
            low = low + strip_wide(ra[h, sl, :]) * cv[h, SIGMA, 0:1, cs]
            bb[sl, cs] = (dd[h, sl, cs] - kk[h, sl, cs] * low).astype(BF16)
            return c

        strips(body)
        by_columns(qt, dk, h)
        rs_start(1, h, dk)
        res = jnp.dot(bb[...], k[:, head(h)], preferred_element_type=F32)
        for b in range(blocks):
            dq[h, b] = res[b * LANES : (b + 1) * LANES]
        start(sq_copies(h))

    def query_last(h):
        arrive(sq_copies(h))
        total = dq[h, ka]
        for n in range(7):
            total = total + sq[h, n]
        gq_ref[:, head(h)] = total * HD**-0.5

    rs_middle(0, 0, dv)
    rs_middle(0, 1, dv)
    rs_middle(1, 0, dk)
    rs_last(0, 0, 1.0, gv_ref)
    query_last(0)
    for h in range(HEADS):
        for r in range(4):
            drain(ka_copies(r, h))
        for r in range(3):
            drain(pb_copies(r, h))
        for e in range(2):
            drain(rs_first(0, h, e, dv))
        drain(sq_copies(h))
    for e in range(2):
        drain(rs_first(1, 0, e, dk))
    rs_middle(1, 1, dk)
    for e in range(2):
        drain(rs_first(1, 1, e, dk))
    rs_last(0, 1, 1.0, gv_ref)
    rs_last(1, 0, HD**-0.5, gk_ref)
    query_last(1)
    rs_last(1, 1, HD**-0.5, gk_ref)

    for h in range(HEADS):
        for w in range(2):
            for e in range(2):
                drain(rs_second(w, h, e))


def settle(*refs):
    count = len(refs) // 2
    for n in range(count):
        refs[count + n][...] = refs[n][...]


def shards(queries, keys, values, grad_out, key_lengths):
    rows, width = queries.shape
    cols = keys.shape[0]
    vmem = lambda *shape: pltpu.VMEM(shape, F32)
    half = lambda *shape: pltpu.VMEM(shape, BF16)
    dma = lambda *shape: pltpu.SemaphoreType.DMA(shape)
    scratch = [
        half(rows, width), half(cols, width), half(cols, width), half(rows, width),
        half(HEADS, HD, rows), half(HEADS, HD, rows),
        vmem(HEADS, rows, cols), vmem(HEADS, rows, cols), half(rows, cols),
        vmem(HEADS, rows, LANES), vmem(HEADS, rows, LANES),
        vmem(HEADS, rows, LANES), vmem(HEADS, rows, LANES),
        vmem(HEADS, 6, 8, cols), vmem(HEADS, 2, cols // LANES, LANES),
        vmem(4, HEADS, 8, 2, rows // LANES, LANES),
        vmem(3, HEADS, 16, 2, cols // LANES, LANES),
        vmem(HEADS, 4, 4, HD, LANES), vmem(HEADS, 4, 4, HD, LANES),
        vmem(HEADS, rows // LANES, LANES, HD),
        vmem(2, HEADS, 2, 3, 4, HD // 2, LANES), vmem(2, HEADS, 2, 4, HD // 2, LANES),
        vmem(2, HEADS, 2, 3, HD // 2, LANES), vmem(HEADS, 7, LANES, HD),
        dma(4), dma(4, HEADS, 7), dma(4, HEADS, 7), dma(3, HEADS, 15), dma(3, HEADS, 15),
        dma(2, HEADS, 2, 3), dma(2, HEADS, 2, 3), dma(2, HEADS, 2, 3), dma(2, HEADS, 2, 3),
        dma(HEADS, 7), dma(HEADS, 7),
    ]
    hbm = pl.BlockSpec(memory_space=pl.ANY)
    here = pl.BlockSpec(memory_space=pltpu.VMEM)
    results = pl.pallas_call(
        functools.partial(kernel, rows, cols),
        out_shape=(
            jax.ShapeDtypeStruct((rows // 8, width), F32),
            jax.ShapeDtypeStruct((cols // 16, width), F32),
            jax.ShapeDtypeStruct((cols // 16, width), F32),
        ),
        in_specs=[pl.BlockSpec(memory_space=pltpu.SMEM), hbm, hbm, hbm, hbm],
        out_specs=(here, here, here),
        scratch_shapes=scratch,
        compiler_params=pltpu.CompilerParams(
            collective_id=0, has_side_effects=True, vmem_limit_bytes=60 * 2**20
        ),
        cost_estimate=pl.CostEstimate(
            flops=24 * rows * cols * HD, bytes_accessed=2**22, transcendentals=4 * rows * cols
        ),
    )(key_lengths, queries, keys, values, grad_out)
    return pl.pallas_call(
        settle,
        out_shape=tuple(jax.ShapeDtypeStruct(r.shape, F32) for r in results),
        in_specs=[here] * 3,
        out_specs=(here,) * 3,
    )(*results)


def solution(mesh):
    placed = (P("pb", None), P("ka", None), P("ka", None), P("pb", None), P("ka"))
    return jax.shard_map(
        shards,
        mesh=mesh,
        in_specs=placed,
        out_specs=(P(("pb", "ka"), None), P(("ka", "pb"), None), P(("ka", "pb"), None)),
        check_vma=False,
    )
```
